32 devices in a mesh: space: 16 (over z, y, core), chan: 2 (over x).
Axes of the slice: x: 2, y: 2, z: 4, core: 2. Of those that a mesh axis runs over, the one named last changes fastest.
Arguments:
- activations: bfloat16 [256, 16, 4096], P('chan', 'space'), may hold values from -6 to 6
- filters: bfloat16 [256, 27, 256], P('chan'), may hold values from -0.078125 to 0.078125
- cotangent: bfloat16 [256, 16, 4096], P('chan', 'space'), may hold values from -6 to 6
Outputs:
- output: bfloat16 [256, 16, 4096], P('chan', 'space')
- input_grad: bfloat16 [256, 16, 4096], P('chan', 'space')
- filter_grad: float32 [256, 27, 256], P('chan')
The draws below stay inside these ranges and needn't reach their ends.
All inputs are finite; a program needn't handle non-finite values.
Results may differ from the reference program's by a relative error of at most 0.001.
Values may be sent and summed in bfloat16 or wider, within the bound.
A program may use at most 192 MiB of HBM per device.

```python
import math
import jax
import jax.numpy as jnp
from jax import lax

CIN = 256
COUT = 256
HGT = 64
WID = 64
TAPS = 27
DEPTH = 16
PLANE = 4096


def steps_of(rng, shape, shards, smallest, top_value):
    def one(axis_at, shards_of):
        draws = jax.random.uniform(jax.random.fold_in(jax.random.fold_in(rng, 6), axis_at), (shards_of,), jnp.float32, smallest / len(shards), top_value / len(shards))
        return jnp.repeat(jnp.exp(draws), shape[axis_at] // shards_of).reshape((-1,) + (1,) * (len(shape) - axis_at - 1))

    loudness = one(*shards[0])
    for cut in shards[1:]:
        loudness = loudness * one(*cut)
    return loudness


def normal_values(rng, dims, deviation, reach, shards=(), kind=jnp.bfloat16):
    level = steps_of(rng, dims, shards, -0.22, 0.18) if shards else 1.0
    entries = jax.random.normal(rng, dims, jnp.float32) * deviation * level
    return jnp.minimum(jnp.maximum(entries, -reach), reach).astype(kind)


def setup_inputs(seed: int = 0) -> dict:
    arg_keys = jax.random.split(jax.random.key(seed), 4)
    activations = normal_values(arg_keys[0], (CIN, DEPTH, PLANE), 1.0, 6.0, ((0, 2), (1, 16)))
    filters = normal_values(arg_keys[1], (COUT, TAPS, CIN), (TAPS * CIN) ** -0.5, 0.078125, ((0, 2),))
    cotangent = normal_values(arg_keys[2], (COUT, DEPTH, PLANE), 1.0, 6.0, ((0, 2), (1, 16)))
    return dict(activations=activations, filters=filters, cotangent=cotangent)


def convolve(volume, kernel):
    return lax.conv_general_dilated(volume, kernel, (1, 1, 1), ((1, 1), (1, 1), (1, 1)), dimension_numbers=('NCDHW', 'OIDHW', 'NCDHW'), precision=lax.Precision.HIGHEST)

def reference(activations, filters, cotangent):
    volume = activations.astype(jnp.float32).reshape(1, CIN, DEPTH, HGT, WID)
    kernel = filters.astype(jnp.float32).reshape(COUT, 3, 3, 3, CIN).transpose(0, 4, 1, 2, 3)
    result, pullback = jax.vjp(convolve, volume, kernel)
    upstream = cotangent.astype(jnp.float32).reshape(1, COUT, DEPTH, HGT, WID)
    volume_grad, kernel_grad = pullback(upstream)
    output = result.reshape(COUT, DEPTH, PLANE).astype(jnp.bfloat16)
    input_grad = volume_grad.reshape(CIN, DEPTH, PLANE).astype(jnp.bfloat16)
    scale = 1.0 / math.sqrt(DEPTH * HGT * WID)
    filter_grad = kernel_grad.transpose(0, 2, 3, 4, 1).reshape(COUT, TAPS, CIN) * scale
    return (output, input_grad, filter_grad.astype(jnp.float32))
```

```python
import math

import jax
import jax.numpy as jnp
from jax import lax
from jax.experimental import pallas as pl
from jax.experimental.pallas import tpu as pltpu
from jax.sharding import PartitionSpec as P

HGT = 64
WID = 64


def swap(value, axis, bit):
    count = lax.axis_size(axis)
    return lax.ppermute(value, axis, [(i, i ^ (1 << bit)) for i in range(count)])


def outward(value, axis):
    count = lax.axis_size(axis)
    pairs = []
    for i in range(count):
        j = i + 1 if i % 2 else i - 1
        if 0 <= j < count:
            pairs.append((i, j))
    return lax.ppermute(value, axis, pairs)


def sum_over(value, axis, bits):
    me = lax.axis_index(axis)
    rows = value.shape[0]
    for bit in bits:
        half = rows // 2
        mine = (me >> bit) & 1
        keep = lax.dynamic_slice_in_dim(value, mine * half, half, 0)
        send = lax.dynamic_slice_in_dim(value, (1 - mine) * half, half, 0)
        value = keep + swap(send, axis, bit)
        rows = half
    for bit in reversed(bits):
        mine = (me >> bit) & 1
        other = swap(value, axis, bit)
        low = jnp.where(mine == 0, value, other)
        high = jnp.where(mine == 0, other, value)
        value = jnp.concatenate([low, high], axis=0)
    return value


def fill_taps(cells, taps):
    count, plane = cells.shape
    tile = 128
    wide = cells.astype(jnp.float32)
    lane = lax.broadcasted_iota(jnp.int32, (count, plane), 1)
    col = lane % WID
    first = lax.broadcasted_iota(jnp.int32, (count, tile), 1) < WID
    for at, step in enumerate((-1, 0, 1)):
        if step == 0:
            moved = wide
        else:
            ok = col > 0 if step == -1 else col < WID - 1
            moved = jnp.where(ok, pltpu.roll(wide, (-step) % plane, 1), 0.0)
        turned = pltpu.roll(moved, WID, 1)
        kind = taps.dtype
        low = turned[:, :tile]
        taps[pl.ds((3 + at) * count, count), :] = moved.astype(kind)
        up = pl.ds(at * count, count)
        taps[up, 0:tile] = jnp.where(first, 0.0, low).astype(kind)
        taps[up, tile:plane] = turned[:, tile:].astype(kind)
        down = pl.ds((6 + at) * count, count)
        taps[down, 0 : plane - tile] = turned[:, tile:].astype(kind)
        taps[down, plane - tile : plane] = jnp.where(first, low, 0.0).astype(kind)


def conv_kernel(width, volume, weights, out, taps, total):
    depth = pl.program_id(0)
    fill_taps(volume[0], taps)

    @pl.loop(0, out.shape[1] // width)
    def _(i):
        at = pl.ds(pl.multiple_of(i * width, width), width)
        part = jnp.dot(weights[0], taps[:, at], preferred_element_type=jnp.float32)

        @pl.when(depth == 0)
        def _():
            total[:, at] = part

        @pl.when(depth > 0)
        def _():
            total[:, at] += part

        @pl.when(depth == 2)
        def _():
            out[:, at] = total[:, at].astype(out.dtype)


def conv(volume, weights, kind):
    _, count, plane = volume.shape
    rows = weights.shape[1]
    return pl.pallas_call(
        lambda *refs: conv_kernel(512, *refs),
        grid=(3,),
        in_specs=[
            pl.BlockSpec((1, count, plane), lambda a: (a, 0, 0)),
            pl.BlockSpec((1, rows, 9 * count), lambda a: (a, 0, 0)),
        ],
        out_specs=pl.BlockSpec((rows, plane), lambda a: (0, 0)),
        out_shape=jax.ShapeDtypeStruct((rows, plane), kind),
        scratch_shapes=[
            pltpu.VMEM((9 * count, plane), jnp.bfloat16),
            pltpu.VMEM((rows, plane), jnp.float32),
        ],
        compiler_params=pltpu.CompilerParams(vmem_limit_bytes=50 << 20),
        cost_estimate=pl.CostEstimate(
            flops=2 * rows * 27 * count * plane,
            bytes_accessed=3 * count * plane * 2 + rows * plane * 4,
            transcendentals=0,
        ),
    )(volume, weights)


def grad_kernel(scale, width, volume, other, out, taps):
    fill_taps(volume[0], taps)
    out[...] = jnp.zeros_like(out)

    @pl.loop(0, other.shape[0] // width)
    def _(i):
        at = pl.ds(pl.multiple_of(i * width, width), width)
        out[0] += jnp.dot(taps[:, at], other[at, :], preferred_element_type=jnp.float32)

    out[...] = out[...] * scale


def kernel_grad(volume, other, scale):
    _, count, plane = volume.shape
    columns = other.shape[1]
    return pl.pallas_call(
        lambda *refs: grad_kernel(scale, 1024, *refs),
        grid=(3,),
        in_specs=[
            pl.BlockSpec((1, count, plane), lambda a: (a, 0, 0)),
            pl.BlockSpec((plane, columns), lambda a: (0, 0)),
        ],
        out_specs=pl.BlockSpec((1, 9 * count, columns), lambda a: (a, 0, 0)),
        out_shape=jax.ShapeDtypeStruct((3, 9 * count, columns), jnp.float32),
        scratch_shapes=[pltpu.VMEM((9 * count, plane), jnp.bfloat16)],
        compiler_params=pltpu.CompilerParams(vmem_limit_bytes=50 << 20),
        cost_estimate=pl.CostEstimate(
            flops=2 * columns * 27 * count * plane,
            bytes_accessed=3 * count * plane * 2 + 27 * count * columns * 4,
            transcendentals=0,
        ),
    )(volume, other)


def per_device(activations, filters, cotangent):
    channels, _, plane = activations.shape
    filter_count, taps, all_channels = filters.shape
    space = lax.axis_size("space")
    me = lax.axis_index("space")
    side = lax.axis_index("chan")
    odd = me % 2
    act = activations[:, 0, :]
    cot = cotangent[:, 0, :]

    def chan_swap(value):
        return lax.ppermute(value, "chan", [(0, 1), (1, 0)])

    def by_channel(own, peer):
        return jnp.where(side == 0, jnp.concatenate([own, peer], 0), jnp.concatenate([peer, own], 0))

    def by_depth(own, inner, outer):
        low = jnp.where(odd == 0, outer, inner)
        high = jnp.where(odd == 0, inner, outer)
        return jnp.stack([low, own, high], axis=0)

    cot_in = swap(cot, "space", 0)
    cot_out = outward(cot, "space")
    act_own = by_channel(act, chan_swap(act))
    cot_volume, act_late, act_own_late = lax.optimization_barrier(
        (by_depth(cot, cot_in, cot_out), act, act_own)
    )
    act_out = outward(act_late, "space")
    act_in = swap(act_own_late, "space", 0)

    scale = 1.0 / math.sqrt(space * plane)
    grad = kernel_grad(cot_volume, act_own.T, scale).reshape(-1, all_channels)
    bits = list(range(space.bit_length() - 1))
    half = all_channels // 2
    first = sum_over(grad[:, :half], "space", bits)
    second = sum_over(grad[:, half:], "space", bits[:1] + bits[2:] + bits[1:2])
    filter_grad = jnp.concatenate([first, second], axis=1).reshape(taps, filter_count, all_channels)
    filter_grad = filter_grad[::-1].transpose(1, 0, 2)

    turned = filters[:, ::-1, :].transpose(2, 1, 0)
    turned = jnp.where(
        side == 0,
        jnp.concatenate([turned[channels:], turned[:channels]], 0),
        turned,
    )
    turned = turned.reshape(all_channels, 3, 9 * filter_count).transpose(1, 0, 2)
    partial = conv(cot_volume, turned, jnp.float32)
    input_grad = partial[channels:] + chan_swap(partial[:channels])
    input_grad = input_grad.astype(jnp.bfloat16).reshape(channels, 1, plane)

    act_volume = by_depth(act_own, act_in, by_channel(act_out, chan_swap(act_out)))
    straight = filters.reshape(filter_count, 3, 9 * all_channels).transpose(1, 0, 2)
    output = conv(act_volume, straight, jnp.bfloat16).reshape(filter_count, 1, plane)
    return (output, input_grad, filter_grad)


def solution(mesh):
    in_specs = (P("chan", "space", None), P("chan", None, None), P("chan", "space", None))
    out_specs = (P("chan", "space", None), P("chan", "space", None), P("chan", None, None))
    return jax.shard_map(
        per_device, mesh=mesh, in_specs=in_specs, out_specs=out_specs, check_vma=False
    )
```
